32 devices in a mesh: groups: 2 (over y), expert: 4 (over z), tensor: 4 (over x, core).
Axes of the slice: x: 2, y: 2, z: 4, core: 2. Of those that a mesh axis runs over, the one named last changes fastest.
Arguments:
- mixer_input: bfloat16 [64, 512], P('groups', ('expert', 'tensor')), parts along dimension 0, may hold values from -6 to 6
- mixer_gate: bfloat16 [64, 512], P('groups', ('expert', 'tensor')), parts along dimension 0, may hold values from -6 to 6
- conv_state: bfloat16 [16, 3, 512], P('groups', None, ('expert', 'tensor')), parts along dimension 0, may hold values from -6 to 6
- conv_weight: float32 [4, 512], P(None, ('expert', 'tensor')), may hold values from -3 to 3
- conv_bias: float32 [512], P(('expert', 'tensor')), may hold values from -3 to 3
- ssm_state: float32 [16, 16, 512], P('groups', None, ('expert', 'tensor')), parts along dimension 0, may hold values from -6 to 6
- decay_rate: float32 [16, 512], P(None, ('expert', 'tensor')), may hold values from 0.01 to 2
- step_bias: float32 [512], P(('expert', 'tensor')), may hold values from -4 to -1
- skip_gain: float32 [512], P(('expert', 'tensor')), may hold values from 0.5 to 1.5
- state_proj: bfloat16 [512, 288], P(('expert', 'tensor')), may hold values from -0.25 to 0.25
- step_proj: bfloat16 [256, 512], P(None, ('expert', 'tensor')), may hold values from -0.375 to 0.375
- out_proj: bfloat16 [512, 4096], P('expert', 'tensor'), may hold values from -0.25 to 0.25
- residual: bfloat16 [64, 4096], P(('groups', 'expert'), 'tensor'), parts along dimension 0, may hold values from -6 to 6
- norm_gain: float32 [4096], P('tensor'), may hold values from 0.5 to 1.5
- expert_gate: bfloat16 [4096, 32768], P(None, ('expert', 'tensor')), may hold values from -0.09375 to 0.09375
- expert_up: bfloat16 [4096, 32768], P(None, ('expert', 'tensor')), may hold values from -0.09375 to 0.09375
- expert_down: bfloat16 [32768, 4096], P(('expert', 'tensor')), may hold values from -0.046875 to 0.046875
- expert_ids: int32 [64, 2], P(('groups', 'expert')), parts along dimension 0, may hold values from 0 to 15, as said below
- route_gates: float32 [64, 2], P(('groups', 'expert')), parts along dimension 0, may hold values from 0.1 to 1
- request_lengths: int32 [16], P('groups'), parts along dimension 0, may hold values from 1 to 8, 32 in all
Outputs:
- layer_out: bfloat16 [64, 4096], P(('groups', 'expert'), 'tensor'), parts along dimension 0
- final_state: float32 [16, 16, 512], P('groups', None, ('expert', 'tensor')), parts along dimension 0
The draws below stay inside these ranges and needn't reach their ends.
There are 2 independent parts, one for each index of `groups`. The reference program is written for one: setup_inputs(seed, part) draws one part's arguments, and reference() takes and returns one part's arrays. A program takes and returns all parts, laid end to end along the dimension named above; an argument that names none is the same for every part. Nothing has to cross between parts.
Inputs may be any that keep to these rules, and one draw needn't show every extreme that they name: `expert_ids`: each row names two different experts. Within each aligned block of 8 rows, each expert below 2 is named by at least one and at most 2 rows; one of them is named by exactly 2 rows in every block.
All inputs are finite; a program needn't handle non-finite values.
Results may differ from the reference program's by a relative error of at most 0.0057.
Values may be sent and summed in bfloat16 or wider, within the bound.
A program may use at most 128 MiB of HBM per device.

```python
import math
import jax
import jax.numpy as jnp
import numpy as np
from jax import lax

D = 4096
NSTATE = 16
DT_RANK = 256
CONV = 4
EXPERTS = 16
EXP_WIN = 2
FF = 16384
REQ = 8
TOK_DEV = 8
TOKENS = 32
CAP = 2
E_INNER = 512
XW = 288
N_EXPERT = 4


def draw_expert_ids(key, part):
    key = jax.random.fold_in(key, 11)
    subkeys = jax.random.split(key, 7)
    blocks = TOKENS // TOK_DEV
    counts = jax.random.randint(subkeys[0], (blocks, EXP_WIN), 1, CAP + 1)
    busiest = jax.random.randint(subkeys[1], (), 0, EXP_WIN)
    peak_block = jax.random.randint(subkeys[2], (EXP_WIN,), 0, blocks)
    block_index = jnp.arange(blocks)[:, None]
    expert_cols = jnp.arange(EXP_WIN)[None, :]
    counts = jnp.where((expert_cols == busiest) | (block_index == peak_block[None, :]), CAP, counts)
    orders = jax.vmap(lambda sub_key: jax.random.permutation(sub_key, TOK_DEV))(jax.random.split(subkeys[3], blocks))
    rank_pos = jnp.argsort(orders, axis=1)
    window_pick = rank_pos // CAP
    within = rank_pos % CAP
    clipped = jnp.minimum(window_pick, EXP_WIN - 1)
    limit_count = jnp.take_along_axis(counts, clipped, axis=1)
    chosen = (window_pick < EXP_WIN) & (within < limit_count)
    spread = EXPERTS - EXP_WIN
    first_other = jax.random.randint(subkeys[4], (blocks, TOK_DEV), 0, spread)
    offset_other = jax.random.randint(subkeys[5], (blocks, TOK_DEV), 1, spread)
    second_other = (first_other + offset_other) % spread
    slot_side = jax.random.randint(subkeys[6], (blocks, TOK_DEV), 0, 2)
    first_col = jnp.where(chosen & (slot_side == 0), window_pick, first_other + EXP_WIN)
    second_col = jnp.where(chosen & (slot_side == 1), window_pick, second_other + EXP_WIN)
    return jnp.stack([first_col, second_col], axis=-1).reshape(TOKENS, 2).astype(jnp.int32)


def steps_of(stream_key, shape, shards, smallest, high):
    factor_of = 1.0
    for axis_at, parts in shards:
        draws = jax.random.uniform(jax.random.fold_in(jax.random.fold_in(stream_key, 6), axis_at), (parts,), jnp.float32, smallest / len(shards), high / len(shards))
        factor_of = factor_of * jnp.repeat(jnp.exp(draws), shape[axis_at] // parts).reshape((-1,) + (1,) * (len(shape) - 1 - axis_at))
    return factor_of


def split_up(number_of, total, limit, slope):
    loads = [(1 << 20) // math.isqrt(standing ** slope) + 1 for standing in range(2, number_of + 1)]
    rest, given = total - limit - (number_of - 1), [1] * (number_of - 1)
    while rest > 0:
        candidates = [i for i in range(number_of - 1) if given[i] < limit]
        mass, remaining = sum([loads[i] for i in candidates]), rest
        for i in candidates:
            addition = min(limit - given[i], max(1, remaining * loads[i] // mass), rest)
            given[i] = given[i] + addition
            rest = rest - addition
    return np.array([limit] + given)


def ragged_sizes(key, number_of, total, reach, skew):
    if number_of == 2:
        one = jax.random.randint(key, (), max(1, total - reach), min(reach, total - 1) + 1)
        return jnp.stack([one, total - one])
    lengths = jnp.asarray(split_up(number_of, total, reach, skew), jnp.int32)
    twos = (number_of - 1) // 2
    giver, sink = lengths[1:1 + 2 * twos:2], lengths[2:2 + 2 * twos:2]
    margin = jnp.minimum(giver - 1, reach - sink)
    moved = jax.random.randint(jax.random.fold_in(key, 1), (twos,), 0, 1 << 20) % (margin + 1)
    lengths = lengths.at[1:1 + 2 * twos:2].set(giver - moved).at[2:2 + 2 * twos:2].set(sink + moved)
    return lengths[jax.random.permutation(jax.random.fold_in(key, 2), number_of)]


def bell_draw(rng, shape, scale, bound, shards=(), held_as=jnp.bfloat16):
    values = scale * jax.random.normal(rng, shape, jnp.float32)
    if shards:
        values = values * steps_of(rng, shape, shards, -0.22, 0.18)
    return jnp.clip(values, -bound, bound).astype(held_as)


def setup_inputs(seed: int = 0, part: int = 0) -> dict:
    streams_of = jax.random.split(jax.random.key(seed), 21)
    part_keys = jax.random.split(jax.random.fold_in(streams_of[20], part), 21)
    mixer_input = bell_draw(part_keys[0], (TOKENS, E_INNER), 1.0, 6.0, ((1, 16),))
    mixer_gate = bell_draw(part_keys[1], (TOKENS, E_INNER), 1.0, 6.0, ((1, 16),))
    conv_state = bell_draw(part_keys[2], (REQ, CONV - 1, E_INNER), 1.0, 6.0, ((2, 16),))
    conv_weight = bell_draw(streams_of[3], (CONV, E_INNER), CONV ** -0.5, 3.0, ((1, 16),), jnp.float32)
    conv_bias = bell_draw(streams_of[4], (E_INNER,), 0.5, 3.0, ((0, 16),), jnp.float32)
    ssm_state = bell_draw(part_keys[5], (REQ, NSTATE, E_INNER), 1.0, 6.0, ((2, 16),), jnp.float32)
    decay_rate = jnp.clip(jnp.exp(math.log(2.0) - 5.2983174 * jax.random.uniform(streams_of[6], (NSTATE, E_INNER), jnp.float32) ** steps_of(streams_of[6], (NSTATE, E_INNER), ((1, 16),), -0.2, 0.2)), 0.01, 2.0)
    step_bias = jnp.clip(-4.0 + 3.0 * jax.random.uniform(streams_of[7], (E_INNER,), jnp.float32) ** steps_of(streams_of[7], (E_INNER,), ((0, 16),), -0.2, 0.2), -4.0, -1.0)
    skip_gain = jnp.clip(0.5 + 1.0 * jax.random.uniform(streams_of[8], (E_INNER,), jnp.float32) ** steps_of(streams_of[8], (E_INNER,), ((0, 16),), -0.2, 0.2), 0.5, 1.5)
    state_proj = bell_draw(streams_of[9], (E_INNER, XW), E_INNER ** -0.5, 0.25, ((0, 16),))
    step_proj = bell_draw(streams_of[10], (DT_RANK, E_INNER), DT_RANK ** -0.5, 0.375, ((1, 16),))
    out_proj = bell_draw(streams_of[11], (E_INNER, D), E_INNER ** -0.5, 0.25, ((0, 4), (1, 4)))
    residual = bell_draw(part_keys[12], (TOKENS, D), 1.0, 6.0, ((0, 4), (1, 4)))
    norm_gain = jnp.clip(1.0 + 0.1 * jax.random.normal(streams_of[13], (D,), jnp.float32), 0.5, 1.5)
    expert_gate = bell_draw(streams_of[14], (D, EXP_WIN * FF), D ** -0.5, 0.09375, ((1, 16),))
    expert_up = bell_draw(streams_of[15], (D, EXP_WIN * FF), D ** -0.5, 0.09375, ((1, 16),))
    expert_down = bell_draw(streams_of[16], (EXP_WIN * FF, D), FF ** -0.5, 0.046875, ((0, 16),))
    expert_ids = draw_expert_ids(jax.random.fold_in(jax.random.fold_in(streams_of[20], part), 71), part)
    route_gates = jnp.clip(0.1 + 0.9 * jax.random.uniform(part_keys[18], (TOKENS, 2), jnp.float32) ** steps_of(part_keys[18], (TOKENS, 2), ((0, 4),), -0.2, 0.2), 0.1, 1.0)
    request_lengths = ragged_sizes(part_keys[19], REQ, TOKENS, TOKENS // 4, 2).astype(jnp.int32)
    return dict(mixer_input=mixer_input, mixer_gate=mixer_gate, conv_state=conv_state, conv_weight=conv_weight, conv_bias=conv_bias, ssm_state=ssm_state, decay_rate=decay_rate, step_bias=step_bias, skip_gain=skip_gain, state_proj=state_proj, step_proj=step_proj, out_proj=out_proj, residual=residual, norm_gain=norm_gain, expert_gate=expert_gate, expert_up=expert_up, expert_down=expert_down, expert_ids=expert_ids, route_gates=route_gates, request_lengths=request_lengths)


EPSILON = 1e-05

def convolve(mixer_input, conv_state, conv_weight, conv_bias, request_lengths):
    total_rows = mixer_input.shape[0]
    request_ends = jnp.cumsum(request_lengths).astype(jnp.int32)
    request_starts = (request_ends - request_lengths).astype(jnp.int32)
    places = jnp.arange(total_rows, dtype=jnp.int32)
    request = lax.optimization_barrier(jnp.sum((places[:, None] >= request_ends[None, :]).astype(jnp.int32), axis=1)).astype(jnp.int32)
    first_pos = jnp.take(request_starts, request).astype(jnp.int32)
    kernel_width = conv_weight.shape[0]
    summed = jnp.zeros(mixer_input.shape, jnp.float32) + conv_bias[None, :].astype(jnp.float32)
    for tap_index in range(kernel_width):
        shift_back = kernel_width - 1 - tap_index
        source = places - shift_back
        inside = source >= first_pos
        from_span = jnp.take(mixer_input, jnp.maximum(source, 0).astype(jnp.int32), axis=0).astype(jnp.float32)
        state_slot = jnp.clip(source - first_pos + kernel_width - 1, 0, kernel_width - 2).astype(jnp.int32)
        from_state = conv_state[request, state_slot].astype(jnp.float32)
        summed = summed + conv_weight[tap_index][None, :] * jnp.where(inside[:, None], from_span, from_state)
    return (jax.nn.silu(summed).astype(jnp.bfloat16), request, first_pos, request_ends)

def reference(mixer_input, mixer_gate, conv_state, conv_weight, conv_bias, ssm_state, decay_rate, step_bias, skip_gain, state_proj, step_proj, out_proj, residual, norm_gain, expert_gate, expert_up, expert_down, expert_ids, route_gates, request_lengths):
    conv_out, request, first_pos, request_ends = convolve(mixer_input, conv_state, conv_weight, conv_bias, request_lengths)
    projected = jnp.dot(conv_out, state_proj, preferred_element_type=jnp.float32)
    step_low = projected[:, :DT_RANK].astype(jnp.bfloat16)
    input_map = projected[:, DT_RANK:DT_RANK + NSTATE]
    output_map = projected[:, DT_RANK + NSTATE:]
    step_size = jax.nn.softplus(jnp.dot(step_low, step_proj, preferred_element_type=jnp.float32) + step_bias[None, :])
    conv_float = conv_out.astype(jnp.float32)
    places = jnp.arange(TOKENS, dtype=jnp.int32)
    opening = places == first_pos
    closing = places == jnp.take(request_ends, request) - 1

    def advance(scan_carry, scan_item):
        state_now, final_now = scan_carry
        step_row, input_row, map_in, map_out, request_now, is_open, is_close = scan_item
        before = jnp.where(is_open, ssm_state[request_now], state_now)
        state_next = jnp.exp(-step_row[None, :] * decay_rate) * before + (step_row * input_row)[None, :] * map_in[:, None]
        emitted = lax.optimization_barrier(jnp.sum(map_out[:, None] * state_next, axis=0))
        kept_state = jnp.where(is_close, state_next, final_now[request_now])
        final_now = final_now.at[request_now].set(kept_state)
        return ((state_next, final_now), emitted)
    start_state = jnp.zeros(ssm_state.shape[1:], jnp.float32)
    start_final = jnp.zeros(ssm_state.shape, jnp.float32)
    carried, scanned = lax.scan(advance, (start_state, start_final), (step_size, conv_float, input_map, output_map, request, opening, closing))
    final_state = carried[1]
    mixed_out = ((scanned + skip_gain[None, :] * conv_float) * jax.nn.silu(mixer_gate.astype(jnp.float32))).astype(jnp.bfloat16)
    stream = residual.astype(jnp.float32) + jnp.dot(mixed_out, out_proj, preferred_element_type=jnp.float32)
    mean_square = lax.optimization_barrier(jnp.mean(stream * stream, axis=1))
    normed = (stream * lax.rsqrt(mean_square + EPSILON)[:, None] * norm_gain[None, :]).astype(jnp.bfloat16)
    expert_sum = jnp.zeros((TOKENS, D), jnp.float32)
    slot_total = N_EXPERT * CAP
    for window_expert in range(EXP_WIN):
        named_here = expert_ids == window_expert
        member = jnp.any(named_here, axis=1)
        weight = lax.optimization_barrier(jnp.sum(jnp.where(named_here, route_gates, 0.0), axis=1))
        token_rows = jnp.nonzero(member, size=slot_total, fill_value=0)[0].astype(jnp.int32)
        live_rows = jnp.arange(slot_total) < jnp.sum(member.astype(jnp.int32))
        chosen = jnp.take(normed, token_rows, axis=0)
        gate_part = jnp.dot(chosen, expert_gate[:, window_expert * FF:(window_expert + 1) * FF], preferred_element_type=jnp.float32)
        up_part = jnp.dot(chosen, expert_up[:, window_expert * FF:(window_expert + 1) * FF], preferred_element_type=jnp.float32)
        hidden_act = (jax.nn.silu(gate_part) * up_part).astype(jnp.bfloat16)
        result = jnp.dot(hidden_act, expert_down[window_expert * FF:(window_expert + 1) * FF, :], preferred_element_type=jnp.float32)
        row_scale = jnp.where(live_rows, jnp.take(weight, token_rows), 0.0)
        expert_sum = expert_sum.at[token_rows].add(result * row_scale[:, None])
    layer_out = (stream + expert_sum).astype(jnp.bfloat16)
    return (layer_out, final_state)
```

```python
import functools

import jax
import jax.numpy as jnp
from jax import lax
from jax.experimental import pallas as pl
from jax.experimental.pallas import tpu as pltpu
from jax.sharding import PartitionSpec as P

EXP_WIN = 2
CAP = 2
EPSILON = 1e-05
LANES = 128
MESH = pl.DeviceIdType.MESH
F32 = jnp.float32
BF16 = jnp.bfloat16


def silu(u):
    return u / (1.0 + jnp.exp(-u))


def kernel(
    n_expert,
    n_tensor,
    lengths_ref,
    ids_ref,
    gates_ref,
    mixer_input,
    mixer_gate,
    conv_state,
    conv_weight,
    conv_bias,
    ssm_state,
    decay_rate,
    step_bias,
    skip_gain,
    state_proj,
    step_proj,
    out_proj,
    residual,
    norm_gain,
    gate_hbm,
    up_hbm,
    down_hbm,
    layer_out,
    final_state,
    gate_v,
    up_v,
    down_v,
    shifted,
    part_send,
    part_recv,
    proj_send,
    proj_recv,
    proj_all,
    decay_all,
    drive_all,
    carried,
    mixed_all,
    mix_send,
    mix_recv,
    stream_s,
    tok_send,
    tok_recv,
    tokens_s,
    hidden,
    out_send,
    out_recv,
    load_sem,
    s1,
    r1,
    s2,
    r2,
    s3,
    r3,
    s4,
    r4,
    s5,
    r5,
    s6,
    r6,
):
    n_all = n_expert * n_tensor
    my_e = lax.axis_index("expert")
    my_t = lax.axis_index("tensor")
    me = my_e * n_tensor + my_t
    total, chans = mixer_input.shape
    requests = conv_state.shape[0]
    taps = conv_weight.shape[0]
    states = decay_rate.shape[0]
    rank = step_proj.shape[0]
    rows_each = total // n_all
    toks, feats = residual.shape
    width = feats * n_tensor
    group = n_expert // EXP_WIN
    held = n_expert * CAP

    loads = [
        pltpu.make_async_copy(src, dst, load_sem.at[i])
        for i, (src, dst) in enumerate(((gate_hbm, gate_v), (up_hbm, up_v), (down_hbm, down_v)))
    ]
    for load in loads:
        load.start()

    def other(k):
        d = lax.rem(me + k, n_all)
        return d, d // n_tensor, lax.rem(d, n_tensor)

    def at(e, t):
        return {"expert": e, "tensor": t}

    barrier = pltpu.get_barrier_semaphore()

    def greet(k, _):
        d, e, t = other(k)
        pl.semaphore_signal(barrier, inc=1, device_id=at(e, t), device_id_type=MESH)
        return 0

    lax.fori_loop(1, n_all, greet, 0)

    starts, ends = [], []
    run = jnp.int32(0)
    for r in range(requests):
        starts.append(run)
        run = run + lengths_ref[r]
        ends.append(run)
    place = lax.broadcasted_iota(jnp.int32, (total, chans), 0)
    first = jnp.zeros((total, chans), jnp.int32)
    from_state = [jnp.zeros((total, chans), F32) for _ in range(taps - 1)]
    for r in range(requests):
        inside = place >= starts[r]
        first = jnp.where(inside, starts[r], first)
        old = conv_state[r].astype(F32)
        for j in range(taps - 1):
            from_state[j] = jnp.where(inside, old[j : j + 1, :], from_state[j])
    since = place - first
    shifted[0:8, :] = jnp.zeros((8, chans), F32)
    shifted[8:, :] = mixer_input[...].astype(F32)
    summed = jnp.zeros((total, chans), F32) + conv_bias[...]
    for k in range(taps):
        back = taps - 1 - k
        value = shifted[8 - back : 8 - back + total, :]
        if back:
            carried_in = from_state[0]
            for j in range(1, taps - 1):
                carried_in = jnp.where(since - back + taps - 1 == j, from_state[j], carried_in)
            value = jnp.where(since >= back, value, carried_in)
        summed = summed + conv_weight[k : k + 1, :] * value
    conv_out = silu(summed).astype(BF16)
    conv_float = conv_out.astype(F32)

    partial = jnp.dot(conv_out, state_proj[...], preferred_element_type=F32)
    for d in range(n_all):
        part_send[d] = partial[d * rows_each : (d + 1) * rows_each, :]
    part_recv[me] = part_send[me]

    pl.semaphore_wait(barrier, n_all - 1)

    def copy1(k):
        d, e, t = other(k)
        return pltpu.make_async_remote_copy(
            src_ref=part_send.at[d],
            dst_ref=part_recv.at[me],
            send_sem=s1.at[k],
            recv_sem=r1.at[k],
            device_id=at(e, t),
            device_id_type=MESH,
        )

    def copy2(k):
        d, e, t = other(k)
        return pltpu.make_async_remote_copy(
            src_ref=proj_send,
            dst_ref=proj_recv.at[me],
            send_sem=s2.at[k],
            recv_sem=r2.at[k],
            device_id=at(e, t),
            device_id_type=MESH,
        )

    def start_all(copy, count):
        lax.fori_loop(1, count, lambda k, c: (copy(k).start(), c)[1], 0)

    def receive_all(copy, count):
        lax.fori_loop(1, count, lambda k, c: (copy(k).wait_recv(), c)[1], 0)

    def sent_all(copy, count):
        lax.fori_loop(1, count, lambda k, c: (copy(k).wait_send(), c)[1], 0)

    start_all(copy1, n_all)
    receive_all(copy1, n_all)
    proj_send[...] = jnp.sum(part_recv[...], axis=0)
    start_all(copy2, n_all)
    proj_recv[me] = proj_send[...]

    slots = []
    for w in range(EXP_WIN):
        count = jnp.int32(0)
        index = [jnp.int32(0) for _ in range(CAP)]
        weight = [jnp.float32(0) for _ in range(CAP)]
        for row in range(toks):
            zero = ids_ref[row, 0] == w
            one = ids_ref[row, 1] == w
            named = jnp.logical_or(zero, one)
            gate = jnp.where(zero, gates_ref[row, 0], 0.0) + jnp.where(one, gates_ref[row, 1], 0.0)
            for s in range(CAP):
                here = jnp.logical_and(named, count == s)
                index[s] = jnp.where(here, row, index[s])
                weight[s] = jnp.where(here, gate, weight[s])
            count = count + named.astype(jnp.int32)
        slots.append((index, weight))

    receive_all(copy2, n_all)
    for d in range(n_all):
        proj_all[d * rows_each : (d + 1) * rows_each, :] = proj_recv[d]
    projected = proj_all[...]
    step_low = projected[:, :rank].astype(BF16)
    input_map = projected[:, rank : rank + states]
    output_map = projected[:, rank + states :]
    raw = jnp.dot(step_low, step_proj[...], preferred_element_type=F32) + step_bias[...]
    step = jnp.maximum(raw, 0.0) + jnp.log1p(jnp.exp(-jnp.abs(raw)))

    decay_all[...] = jnp.exp(-step[:, None, :] * decay_rate[...][None, :, :])
    drive_all[...] = (step * conv_float)[:, None, :] * input_map[:, :, None]

    def advance(t, carry):
        h, r, begin, end = carry
        before = jnp.where(t == begin, ssm_state[r], h)
        h = decay_all[t] * before + drive_all[t]
        carried[t] = h
        over = t + 1 == end
        following = jnp.minimum(r + 1, requests - 1)
        return (
            h,
            jnp.where(over, following, r),
            jnp.where(over, end, begin),
            jnp.where(over, end + lengths_ref[following], end),
        )

    lax.fori_loop(
        0,
        total,
        advance,
        (jnp.zeros((states, chans), F32), jnp.int32(0), jnp.int32(0), ends[0]),
    )
    for r in range(requests):
        final_state[r] = carried[jnp.clip(ends[r] - 1, 0, total - 1)]
    scanned = jnp.sum(carried[...] * output_map[:, :, None], axis=1)
    mixed = (scanned + skip_gain[...] * conv_float) * silu(mixer_gate[...].astype(F32))
    mixed_all[my_t] = mixed.astype(BF16)

    def copy3(k):
        return pltpu.make_async_remote_copy(
            src_ref=mixed_all.at[my_t],
            dst_ref=mixed_all.at[my_t],
            send_sem=s3.at[k],
            recv_sem=r3.at[k],
            device_id=at(my_e, lax.rem(my_t + k, n_tensor)),
            device_id_type=MESH,
        )

    start_all(copy3, n_tensor)
    receive_all(copy3, n_tensor)
    part = jnp.zeros((total, feats), F32)
    for t in range(n_tensor):
        part = part + jnp.dot(
            mixed_all[t], out_proj[t * chans : (t + 1) * chans, :], preferred_element_type=F32
        )
    half = feats // 2
    for e in range(n_expert):
        rows = part[e * toks : (e + 1) * toks, :]
        mix_send[e] = jnp.concatenate([rows[:, :half], rows[:, half:]], axis=0).astype(BF16)
    mix_recv[my_e] = mix_send[my_e]

    def copy4(k):
        e = lax.rem(my_e + k, n_expert)
        return pltpu.make_async_remote_copy(
            src_ref=mix_send.at[e],
            dst_ref=mix_recv.at[my_e],
            send_sem=s4.at[k],
            recv_sem=r4.at[k],
            device_id=at(e, my_t),
            device_id_type=MESH,
        )

    start_all(copy4, n_expert)
    receive_all(copy4, n_expert)
    mix = jnp.sum(mix_recv[...].astype(F32), axis=0)
    stream = residual[...].astype(F32) + jnp.concatenate([mix[:toks], mix[toks:]], axis=1)
    squares = jnp.sum(stream * stream, axis=1, keepdims=True)
    stream_s[:, :feats] = stream * norm_gain[...]
    stream_s[:, feats:] = jnp.broadcast_to(squares, (toks, LANES))

    for w in range(EXP_WIN):
        for s in range(CAP):
            tok_send[w, s : s + 1, :] = stream_s[pl.ds(slots[w][0][s], 1), :]
    tok_recv[me] = tok_send[my_e // group]

    def copy5(k):
        d, e, t = other(k)
        return pltpu.make_async_remote_copy(
            src_ref=tok_send.at[e // group],
            dst_ref=tok_recv.at[me],
            send_sem=s5.at[k],
            recv_sem=r5.at[k],
            device_id=at(e, t),
            device_id_type=MESH,
        )

    start_all(copy5, n_all)
    receive_all(copy5, n_all)
    padded = tokens_s.shape[0]
    if padded > held:
        tokens_s[held:, :] = jnp.zeros((padded - held, width + LANES), F32)
    for e in range(n_expert):
        square = jnp.zeros((CAP, LANES), F32)
        for t in range(n_tensor):
            got = tok_recv[e * n_tensor + t]
            tokens_s[e * CAP : (e + 1) * CAP, t * feats : (t + 1) * feats] = got[:, :feats]
            square = square + got[:, feats:]
        tokens_s[e * CAP : (e + 1) * CAP, width:] = square
    scale = lax.rsqrt(tokens_s[:, width : width + 1] / width + EPSILON)
    normed = (tokens_s[:, :width] * scale).astype(BF16)

    loads[0].wait()
    loads[1].wait()
    units = gate_v.shape[1]
    tile = 256 if units % 256 == 0 else units

    def unit_tile(i, c):
        cols = pl.ds(pl.multiple_of(i * tile, tile), tile) if units > tile else slice(None)
        g = jnp.dot(normed, gate_v[:, cols], preferred_element_type=F32)
        u = jnp.dot(normed, up_v[:, cols], preferred_element_type=F32)
        hidden[:, cols] = (silu(g) * u).astype(BF16)
        return c

    lax.fori_loop(0, units // tile, unit_tile, 0)
    loads[2].wait()
    act = hidden[...]
    otile = 512 if feats % 512 == 0 else feats

    def out_tile(i, c):
        cols = pl.ds(pl.multiple_of(i * otile, otile), otile)
        got = jnp.dot(act, down_v[:, cols], preferred_element_type=F32)
        for e in range(n_expert):
            out_send[e, :, cols] = got[e * CAP : (e + 1) * CAP, :]
        return c

    def copy6(k):
        d, e, t = other(k)
        return pltpu.make_async_remote_copy(
            src_ref=out_send.at[e, :, pl.ds(pl.multiple_of(t * feats, LANES), feats)],
            dst_ref=out_recv.at[me],
            send_sem=s6.at[k],
            recv_sem=r6.at[k],
            device_id=at(e, t),
            device_id_type=MESH,
        )

    lax.fori_loop(0, width // otile, out_tile, 0)
    start_all(copy6, n_all)
    out_recv[me] = out_send[my_e, :, pl.ds(pl.multiple_of(my_t * feats, LANES), feats)]
    receive_all(copy6, n_all)
    row_id = lax.broadcasted_iota(jnp.int32, (toks, feats), 0)
    result = residual[...].astype(F32) + jnp.concatenate([mix[:toks], mix[toks:]], axis=1)
    share = group * n_tensor
    for w in range(EXP_WIN):
        value = jnp.sum(out_recv[w * share : (w + 1) * share], axis=0)
        for s in range(CAP):
            index, weight = slots[w]
            result = result + jnp.where(row_id == index[s], weight[s], 0.0) * value[s : s + 1, :]
    layer_out[...] = result.astype(BF16)
    for copy, count in (
        (copy1, n_all),
        (copy2, n_all),
        (copy3, n_tensor),
        (copy4, n_expert),
        (copy5, n_all),
        (copy6, n_all),
    ):
        sent_all(copy, count)


def body(
    n_expert,
    n_tensor,
    mixer_input,
    mixer_gate,
    conv_state,
    conv_weight,
    conv_bias,
    ssm_state,
    decay_rate,
    step_bias,
    skip_gain,
    state_proj,
    step_proj,
    out_proj,
    residual,
    norm_gain,
    expert_gate,
    expert_up,
    expert_down,
    expert_ids,
    route_gates,
    request_lengths,
):
    n_all = n_expert * n_tensor
    total, chans = mixer_input.shape
    states = decay_rate.shape[0]
    xw = state_proj.shape[1]
    toks, feats = residual.shape
    width = feats * n_tensor
    rows_each = total // n_all
    held = -(-n_expert * CAP // 16) * 16
    smem = pl.BlockSpec(memory_space=pltpu.SMEM)
    vmem = pl.BlockSpec(memory_space=pltpu.VMEM)
    hbm = pl.BlockSpec(memory_space=pl.ANY)
    sem = pltpu.SemaphoreType.DMA
    return pl.pallas_call(
        functools.partial(kernel, n_expert, n_tensor),
        out_shape=(
            jax.ShapeDtypeStruct((toks, feats), BF16),
            jax.ShapeDtypeStruct(ssm_state.shape, F32),
        ),
        in_specs=[smem] * 3 + [vmem] * 14 + [hbm] * 3,
        out_specs=(vmem, vmem),
        scratch_shapes=[
            pltpu.VMEM(expert_gate.shape, BF16),
            pltpu.VMEM(expert_up.shape, BF16),
            pltpu.VMEM(expert_down.shape, BF16),
            pltpu.VMEM((total + 8, chans), F32),
            pltpu.VMEM((n_all, rows_each, xw), F32),
            pltpu.VMEM((n_all, rows_each, xw), F32),
            pltpu.VMEM((rows_each, xw), F32),
            pltpu.VMEM((n_all, rows_each, xw), F32),
            pltpu.VMEM((total, xw), F32),
            pltpu.VMEM((total, states, chans), F32),
            pltpu.VMEM((total, states, chans), F32),
            pltpu.VMEM((total, states, chans), F32),
            pltpu.VMEM((n_tensor, total, chans), BF16),
            pltpu.VMEM((n_expert, 2 * toks, feats // 2), BF16),
            pltpu.VMEM((n_expert, 2 * toks, feats // 2), BF16),
            pltpu.VMEM((toks, feats + LANES), F32),
            pltpu.VMEM((EXP_WIN, CAP, feats + LANES), F32),
            pltpu.VMEM((n_all, CAP, feats + LANES), F32),
            pltpu.VMEM((held, width + LANES), F32),
            pltpu.VMEM((held, expert_gate.shape[1]), BF16),
            pltpu.VMEM((n_expert, CAP, width), F32),
            pltpu.VMEM((n_all, CAP, feats), F32),
            sem((3,)),
            sem((n_all,)),
            sem((n_all,)),
            sem((n_all,)),
            sem((n_all,)),
            sem((n_tensor,)),
            sem((n_tensor,)),
            sem((n_expert,)),
            sem((n_expert,)),
            sem((n_all,)),
            sem((n_all,)),
            sem((n_all,)),
            sem((n_all,)),
        ],
        compiler_params=pltpu.CompilerParams(
            collective_id=0, has_side_effects=True, vmem_limit_bytes=60 * 1024 * 1024
        ),
    )(
        request_lengths,
        expert_ids,
        route_gates,
        mixer_input,
        mixer_gate,
        conv_state,
        conv_weight,
        conv_bias[None],
        ssm_state,
        decay_rate,
        step_bias[None],
        skip_gain[None],
        state_proj,
        step_proj,
        out_proj,
        residual,
        norm_gain[None],
        expert_gate,
        expert_up,
        expert_down,
    )


def solution(mesh):
    in_specs = (
        P("groups", ("expert", "tensor")),
        P("groups", ("expert", "tensor")),
        P("groups", None, ("expert", "tensor")),
        P(None, ("expert", "tensor")),
        P(("expert", "tensor")),
        P("groups", None, ("expert", "tensor")),
        P(None, ("expert", "tensor")),
        P(("expert", "tensor")),
        P(("expert", "tensor")),
        P(("expert", "tensor"), None),
        P(None, ("expert", "tensor")),
        P("expert", "tensor"),
        P(("groups", "expert"), "tensor"),
        P("tensor"),
        P(None, ("expert", "tensor")),
        P(None, ("expert", "tensor")),
        P(("expert", "tensor"), None),
        P(("groups", "expert"), None),
        P(("groups", "expert"), None),
        P("groups"),
    )
    out_specs = (P(("groups", "expert"), "tensor"), P("groups", None, ("expert", "tensor")))
    run = functools.partial(body, mesh.shape["expert"], mesh.shape["tensor"])
    return jax.shard_map(run, mesh=mesh, in_specs=in_specs, out_specs=out_specs, check_vma=False)
```

```python
import functools

import jax
import jax.numpy as jnp
from jax import lax
from jax.experimental import pallas as pl
from jax.experimental.pallas import tpu as pltpu
from jax.sharding import PartitionSpec as P

EXP_WIN = 2
CAP = 2
EPSILON = 1e-05
LANES = 128
MESH = pl.DeviceIdType.MESH
F32 = jnp.float32
BF16 = jnp.bfloat16


def silu(u):
    return u / (1.0 + jnp.exp(-u))


def kernel(
    n_expert,
    n_tensor,
    lengths_ref,
    ids_ref,
    gates_ref,
    mixer_input,
    mixer_gate,
    conv_state,
    conv_weight,
    conv_bias,
    ssm_state,
    decay_rate,
    step_bias,
    skip_gain,
    state_proj,
    step_proj,
    out_proj,
    residual,
    norm_gain,
    gate_hbm,
    up_hbm,
    down_hbm,
    layer_out,
    final_state,
    gate_v,
    up_v,
    down_v,
    shifted,
    part_send,
    part_recv,
    proj_send,
    proj_recv,
    proj_all,
    decay_all,
    drive_all,
    carried,
    mixed_all,
    mix_send,
    mix_recv,
    stream_s,
    tok_send,
    tok_recv,
    tokens_s,
    hidden,
    out_send,
    out_recv,
    load_sem,
    s1,
    r1,
    s2,
    r2,
    s3,
    r3,
    s4,
    r4,
    s5,
    r5,
    s6,
    r6,
):
    n_all = n_expert * n_tensor
    my_e = lax.axis_index("expert")
    my_t = lax.axis_index("tensor")
    me = my_e * n_tensor + my_t
    total, chans = mixer_input.shape
    requests = conv_state.shape[1]
    taps = conv_weight.shape[0]
    states = decay_rate.shape[0]
    rank = step_proj.shape[1]
    rows_each = total // n_all
    toks, feats = residual.shape
    width = feats * n_tensor
    group = n_expert // EXP_WIN
    held = n_expert * CAP

    loads = [
        pltpu.make_async_copy(src, dst, load_sem.at[i])
        for i, (src, dst) in enumerate(((gate_hbm, gate_v), (up_hbm, up_v), (down_hbm, down_v)))
    ]
    for load in loads:
        load.start()

    def other(k):
        d = lax.rem(me + k, n_all)
        return d, d // n_tensor, lax.rem(d, n_tensor)

    def at(e, t):
        return {"expert": e, "tensor": t}

    barrier = pltpu.get_barrier_semaphore()

    def greet(k, _):
        d, e, t = other(k)
        pl.semaphore_signal(barrier, inc=1, device_id=at(e, t), device_id_type=MESH)
        return 0

    lax.fori_loop(1, n_all, greet, 0)

    starts, ends = [], []
    run = jnp.int32(0)
    for r in range(requests):
        starts.append(run)
        run = run + lengths_ref[r]
        ends.append(run)
    place = lax.broadcasted_iota(jnp.int32, (total, chans), 0)
    first = jnp.zeros((total, chans), jnp.int32)
    old = [conv_state[j].astype(F32) for j in range(taps - 1)]
    from_state = [jnp.zeros((total, chans), F32) for _ in range(taps - 1)]
    for r in range(requests):
        inside = place >= starts[r]
        first = jnp.where(inside, starts[r], first)
        for j in range(taps - 1):
            from_state[j] = jnp.where(inside, old[j][r : r + 1, :], from_state[j])
    since = place - first
    shifted[0:8, :] = jnp.zeros((8, chans), F32)
    shifted[8:, :] = mixer_input[...].astype(F32)
    summed = jnp.zeros((total, chans), F32) + conv_bias[...]
    for k in range(taps):
        back = taps - 1 - k
        value = shifted[8 - back : 8 - back + total, :]
        if back:
            carried_in = from_state[0]
            for j in range(1, taps - 1):
                carried_in = jnp.where(since - back + taps - 1 == j, from_state[j], carried_in)
            value = jnp.where(since >= back, value, carried_in)
        summed = summed + conv_weight[k : k + 1, :] * value
    conv_out = silu(summed).astype(BF16)
    conv_float = conv_out.astype(F32)

    partial = jnp.dot(conv_out, state_proj[...], preferred_element_type=F32)
    for d in range(n_all):
        part_send[d] = partial[d * rows_each : (d + 1) * rows_each, :]
    part_recv[me] = part_send[me]

    pl.semaphore_wait(barrier, n_all - 1)

    def copy1(k):
        d, e, t = other(k)
        return pltpu.make_async_remote_copy(
            src_ref=part_send.at[d],
            dst_ref=part_recv.at[me],
            send_sem=s1.at[k],
            recv_sem=r1.at[k],
            device_id=at(e, t),
            device_id_type=MESH,
        )

    def copy2(k):
        d, e, t = other(k)
        return pltpu.make_async_remote_copy(
            src_ref=proj_send,
            dst_ref=proj_recv.at[me],
            send_sem=s2.at[k],
            recv_sem=r2.at[k],
            device_id=at(e, t),
            device_id_type=MESH,
        )

    def start_all(copy, count):
        lax.fori_loop(1, count, lambda k, c: (copy(k).start(), c)[1], 0)

    def receive_all(copy, count):
        lax.fori_loop(1, count, lambda k, c: (copy(k).wait_recv(), c)[1], 0)

    def sent_all(copy, count):
        lax.fori_loop(1, count, lambda k, c: (copy(k).wait_send(), c)[1], 0)

    start_all(copy1, n_all)
    receive_all(copy1, n_all)
    proj_send[...] = jnp.sum(part_recv[...], axis=0)
    start_all(copy2, n_all)
    proj_recv[me] = proj_send[...]

    slots = []
    for w in range(EXP_WIN):
        count = jnp.int32(0)
        index = [jnp.int32(0) for _ in range(CAP)]
        weight = [jnp.float32(0) for _ in range(CAP)]
        for row in range(toks):
            zero = ids_ref[0, row] == w
            one = ids_ref[1, row] == w
            named = jnp.logical_or(zero, one)
            gate = jnp.where(zero, gates_ref[0, row], 0.0) + jnp.where(one, gates_ref[1, row], 0.0)
            for s in range(CAP):
                here = jnp.logical_and(named, count == s)
                index[s] = jnp.where(here, row, index[s])
                weight[s] = jnp.where(here, gate, weight[s])
            count = count + named.astype(jnp.int32)
        slots.append((index, weight))

    receive_all(copy2, n_all)
    for d in range(n_all):
        proj_all[d * rows_each : (d + 1) * rows_each, :] = proj_recv[d]
    projected = proj_all[...]
    step_low = projected[:, :rank].astype(BF16)
    input_map = projected[:, rank : rank + states]
    output_map = projected[:, rank + states :]
    raw = (
        lax.dot_general(
            step_low, step_proj[...], (((1,), (1,)), ((), ())), preferred_element_type=F32
        )
        + step_bias[...]
    )
    step = jnp.maximum(raw, 0.0) + jnp.log1p(jnp.exp(-jnp.abs(raw)))

    decay_all[...] = jnp.exp(-step[:, None, :] * decay_rate[...][None, :, :])
    drive_all[...] = (step * conv_float)[:, None, :] * input_map[:, :, None]

    def advance(t, carry):
        h, r, begin, end = carry
        before = jnp.where(t == begin, ssm_state[r], h)
        h = decay_all[t] * before + drive_all[t]
        carried[t] = h
        over = t + 1 == end
        following = jnp.minimum(r + 1, requests - 1)
        return (
            h,
            jnp.where(over, following, r),
            jnp.where(over, end, begin),
            jnp.where(over, end + lengths_ref[following], end),
        )

    lax.fori_loop(
        0,
        total,
        advance,
        (jnp.zeros((states, chans), F32), jnp.int32(0), jnp.int32(0), ends[0]),
    )
    for r in range(requests):
        final_state[r] = carried[jnp.clip(ends[r] - 1, 0, total - 1)]
    scanned = jnp.sum(carried[...] * output_map[:, :, None], axis=1)
    mixed = (scanned + skip_gain[...] * conv_float) * silu(mixer_gate[...].astype(F32))
    mixed_all[my_t] = mixed.astype(BF16)

    def copy3(k):
        return pltpu.make_async_remote_copy(
            src_ref=mixed_all.at[my_t],
            dst_ref=mixed_all.at[my_t],
            send_sem=s3.at[k],
            recv_sem=r3.at[k],
            device_id=at(my_e, lax.rem(my_t + k, n_tensor)),
            device_id_type=MESH,
        )

    start_all(copy3, n_tensor)
    receive_all(copy3, n_tensor)
    part = jnp.zeros((total, feats), F32)
    for t in range(n_tensor):
        part = part + jnp.dot(
            mixed_all[t], out_proj[t * chans : (t + 1) * chans, :], preferred_element_type=F32
        )
    half = feats // 2
    for e in range(n_expert):
        rows = part[e * toks : (e + 1) * toks, :]
        mix_send[e] = jnp.concatenate([rows[:, :half], rows[:, half:]], axis=0).astype(BF16)
    mix_recv[my_e] = mix_send[my_e]

    def copy4(k):
        e = lax.rem(my_e + k, n_expert)
        return pltpu.make_async_remote_copy(
            src_ref=mix_send.at[e],
            dst_ref=mix_recv.at[my_e],
            send_sem=s4.at[k],
            recv_sem=r4.at[k],
            device_id=at(e, my_t),
            device_id_type=MESH,
        )

    start_all(copy4, n_expert)
    receive_all(copy4, n_expert)
    mix = jnp.sum(mix_recv[...].astype(F32), axis=0)
    stream = residual[...].astype(F32) + jnp.concatenate([mix[:toks], mix[toks:]], axis=1)
    squares = jnp.sum(stream * stream, axis=1, keepdims=True)
    stream_s[:, :feats] = stream * norm_gain[...]
    stream_s[:, feats:] = jnp.broadcast_to(squares, (toks, LANES))

    for w in range(EXP_WIN):
        for s in range(CAP):
            tok_send[w, s : s + 1, :] = stream_s[pl.ds(slots[w][0][s], 1), :]
    tok_recv[me] = tok_send[my_e // group]

    def copy5(k):
        d, e, t = other(k)
        return pltpu.make_async_remote_copy(
            src_ref=tok_send.at[e // group],
            dst_ref=tok_recv.at[me],
            send_sem=s5.at[k],
            recv_sem=r5.at[k],
            device_id=at(e, t),
            device_id_type=MESH,
        )

    start_all(copy5, n_all)
    receive_all(copy5, n_all)
    padded = tokens_s.shape[0]
    if padded > held:
        tokens_s[held:, :] = jnp.zeros((padded - held, width + LANES), F32)
    for e in range(n_expert):
        square = jnp.zeros((CAP, LANES), F32)
        for t in range(n_tensor):
            got = tok_recv[e * n_tensor + t]
            tokens_s[e * CAP : (e + 1) * CAP, t * feats : (t + 1) * feats] = got[:, :feats]
            square = square + got[:, feats:]
        tokens_s[e * CAP : (e + 1) * CAP, width:] = square
    scale = lax.rsqrt(tokens_s[:, width : width + 1] / width + EPSILON)
    normed = (tokens_s[:, :width] * scale).astype(BF16)

    loads[0].wait()
    loads[1].wait()
    units = gate_v.shape[1]
    tile = 256 if units % 256 == 0 else units

    def unit_tile(i, c):
        cols = pl.ds(pl.multiple_of(i * tile, tile), tile) if units > tile else slice(None)
        g = jnp.dot(normed, gate_v[:, cols], preferred_element_type=F32)
        u = jnp.dot(normed, up_v[:, cols], preferred_element_type=F32)
        hidden[:, cols] = (silu(g) * u).astype(BF16)
        return c

    lax.fori_loop(0, units // tile, unit_tile, 0)
    loads[2].wait()
    act = hidden[...]
    otile = 512 if feats % 512 == 0 else feats

    def out_tile(i, c):
        cols = pl.ds(pl.multiple_of(i * otile, otile), otile)
        got = jnp.dot(act, down_v[:, cols], preferred_element_type=F32)
        for e in range(n_expert):
            out_send[e, :, cols] = got[e * CAP : (e + 1) * CAP, :]
        return c

    def copy6(k):
        d, e, t = other(k)
        return pltpu.make_async_remote_copy(
            src_ref=out_send.at[e, :, pl.ds(pl.multiple_of(t * feats, LANES), feats)],
            dst_ref=out_recv.at[me],
            send_sem=s6.at[k],
            recv_sem=r6.at[k],
            device_id=at(e, t),
            device_id_type=MESH,
        )

    lax.fori_loop(0, width // otile, out_tile, 0)
    start_all(copy6, n_all)
    out_recv[me] = out_send[my_e, :, pl.ds(pl.multiple_of(my_t * feats, LANES), feats)]
    receive_all(copy6, n_all)
    row_id = lax.broadcasted_iota(jnp.int32, (toks, feats), 0)
    result = residual[...].astype(F32) + jnp.concatenate([mix[:toks], mix[toks:]], axis=1)
    share = group * n_tensor
    for w in range(EXP_WIN):
        value = jnp.sum(out_recv[w * share : (w + 1) * share], axis=0)
        for s in range(CAP):
            index, weight = slots[w]
            result = result + jnp.where(row_id == index[s], weight[s], 0.0) * value[s : s + 1, :]
    layer_out[...] = result.astype(BF16)
    for copy, count in (
        (copy1, n_all),
        (copy2, n_all),
        (copy3, n_tensor),
        (copy4, n_expert),
        (copy5, n_all),
        (copy6, n_all),
    ):
        sent_all(copy, count)


def finish(layer_in, state_in, layer_out, final_state):
    layer_out[...] = layer_in[...]
    final_state[...] = state_in[...]


def body(
    n_expert,
    n_tensor,
    mixer_input,
    mixer_gate,
    conv_state,
    conv_weight,
    conv_bias,
    ssm_state,
    decay_rate,
    step_bias,
    skip_gain,
    state_proj,
    step_proj,
    out_proj,
    residual,
    norm_gain,
    expert_gate,
    expert_up,
    expert_down,
    expert_ids,
    route_gates,
    request_lengths,
):
    n_all = n_expert * n_tensor
    total, chans = mixer_input.shape
    states = decay_rate.shape[0]
    xw = state_proj.shape[1]
    toks, feats = residual.shape
    width = feats * n_tensor
    rows_each = total // n_all
    held = -(-n_expert * CAP // 16) * 16
    smem = pl.BlockSpec(memory_space=pltpu.SMEM)
    vmem = pl.BlockSpec(memory_space=pltpu.VMEM)
    hbm = pl.BlockSpec(memory_space=pl.ANY)
    sem = pltpu.SemaphoreType.DMA
    made = pl.pallas_call(
        functools.partial(kernel, n_expert, n_tensor),
        out_shape=(
            jax.ShapeDtypeStruct((toks, feats), BF16),
            jax.ShapeDtypeStruct(ssm_state.shape, F32),
        ),
        in_specs=[smem] * 3 + [vmem] * 14 + [hbm] * 3,
        out_specs=(vmem, vmem),
        scratch_shapes=[
            pltpu.VMEM(expert_gate.shape, BF16),
            pltpu.VMEM(expert_up.shape, BF16),
            pltpu.VMEM(expert_down.shape, BF16),
            pltpu.VMEM((total + 8, chans), F32),
            pltpu.VMEM((n_all, rows_each, xw), F32),
            pltpu.VMEM((n_all, rows_each, xw), F32),
            pltpu.VMEM((rows_each, xw), F32),
            pltpu.VMEM((n_all, rows_each, xw), F32),
            pltpu.VMEM((total, xw), F32),
            pltpu.VMEM((total, states, chans), F32),
            pltpu.VMEM((total, states, chans), F32),
            pltpu.VMEM((total, states, chans), F32),
            pltpu.VMEM((n_tensor, total, chans), BF16),
            pltpu.VMEM((n_expert, 2 * toks, feats // 2), BF16),
            pltpu.VMEM((n_expert, 2 * toks, feats // 2), BF16),
            pltpu.VMEM((toks, feats + LANES), F32),
            pltpu.VMEM((EXP_WIN, CAP, feats + LANES), F32),
            pltpu.VMEM((n_all, CAP, feats + LANES), F32),
            pltpu.VMEM((held, width + LANES), F32),
            pltpu.VMEM((held, expert_gate.shape[1]), BF16),
            pltpu.VMEM((n_expert, CAP, width), F32),
            pltpu.VMEM((n_all, CAP, feats), F32),
            sem((3,)),
            sem((n_all,)),
            sem((n_all,)),
            sem((n_all,)),
            sem((n_all,)),
            sem((n_tensor,)),
            sem((n_tensor,)),
            sem((n_expert,)),
            sem((n_expert,)),
            sem((n_all,)),
            sem((n_all,)),
            sem((n_all,)),
            sem((n_all,)),
        ],
        compiler_params=pltpu.CompilerParams(
            collective_id=0, has_side_effects=True, vmem_limit_bytes=60 * 1024 * 1024
        ),
    )(
        request_lengths,
        expert_ids.T,
        route_gates.T,
        mixer_input,
        mixer_gate,
        conv_state.transpose(1, 0, 2),
        conv_weight,
        conv_bias[None],
        ssm_state,
        decay_rate,
        step_bias[None],
        skip_gain[None],
        state_proj,
        step_proj.T,
        out_proj,
        residual,
        norm_gain[None],
        expert_gate,
        expert_up,
        expert_down,
    )
    return pl.pallas_call(
        finish,
        out_shape=tuple(jax.ShapeDtypeStruct(m.shape, m.dtype) for m in made),
        in_specs=[vmem] * 2,
        out_specs=(vmem, vmem),
    )(*made)


def solution(mesh):
    in_specs = (
        P("groups", ("expert", "tensor")),
        P("groups", ("expert", "tensor")),
        P("groups", None, ("expert", "tensor")),
        P(None, ("expert", "tensor")),
        P(("expert", "tensor")),
        P("groups", None, ("expert", "tensor")),
        P(None, ("expert", "tensor")),
        P(("expert", "tensor")),
        P(("expert", "tensor")),
        P(("expert", "tensor"), None),
        P(None, ("expert", "tensor")),
        P("expert", "tensor"),
        P(("groups", "expert"), "tensor"),
        P("tensor"),
        P(None, ("expert", "tensor")),
        P(None, ("expert", "tensor")),
        P(("expert", "tensor"), None),
        P(("groups", "expert"), None),
        P(("groups", "expert"), None),
        P("groups"),
    )
    out_specs = (P(("groups", "expert"), "tensor"), P("groups", None, ("expert", "tensor")))
    run = functools.partial(body, mesh.shape["expert"], mesh.shape["tensor"])
    return jax.shard_map(run, mesh=mesh, in_specs=in_specs, out_specs=out_specs, check_vma=False)
```

```python
import functools

import jax
import jax.numpy as jnp
from jax import lax
from jax.experimental import pallas as pl
from jax.experimental.pallas import tpu as pltpu
from jax.sharding import PartitionSpec as P

EXP_WIN = 2
CAP = 2
EPSILON = 1e-05
LANES = 128
MESH = pl.DeviceIdType.MESH
F32 = jnp.float32
BF16 = jnp.bfloat16


def silu(u):
    return u / (1.0 + jnp.exp(-u))


def kernel(
    n_expert,
    n_tensor,
    lengths_ref,
    ids_ref,
    gates_ref,
    mixer_input,
    mixer_gate,
    conv_state,
    conv_weight,
    conv_bias,
    ssm_state,
    decay_rate,
    step_bias,
    skip_gain,
    state_proj,
    step_proj,
    out_proj,
    residual,
    norm_gain,
    gate_hbm,
    up_hbm,
    down_hbm,
    layer_out,
    final_state,
    gate_v,
    up_v,
    down_v,
    shifted,
    part_send,
    part_recv,
    proj_send,
    proj_recv,
    proj_all,
    decay_all,
    drive_all,
    carried,
    mixed_all,
    mix_send,
    mix_recv,
    stream_s,
    tok_send,
    tok_held,
    tok_recv,
    tokens_s,
    hidden,
    out_send,
    out_held,
    out_part,
    out_recv,
    load_sem,
    s1,
    r1,
    s2,
    r2,
    s3,
    r3,
    s4,
    r4,
    s5,
    r5,
    s6,
    r6,
    s7,
    r7,
    s8,
    r8,
    s9,
    r9,
):
    my_e = lax.axis_index("expert")
    my_t = lax.axis_index("tensor")
    total, chans = mixer_input.shape
    requests = conv_state.shape[1]
    taps = conv_weight.shape[0]
    states = decay_rate.shape[0]
    rank = step_proj.shape[1]
    rows_each = total // n_tensor
    toks, feats = residual.shape
    width = feats * n_tensor
    group = n_expert // EXP_WIN
    held = n_expert * CAP

    loads = [
        pltpu.make_async_copy(src, dst, load_sem.at[i])
        for i, (src, dst) in enumerate(((gate_hbm, gate_v), (up_hbm, up_v), (down_hbm, down_v)))
    ]
    for load in loads:
        load.start()

    def over_tensor(k):
        return lax.rem(my_t + k, n_tensor)

    def over_expert(k):
        return lax.rem(my_e + k, n_expert)

    def at(e, t):
        return {"expert": e, "tensor": t}

    barrier = pltpu.get_barrier_semaphore()

    def greet_tensor(k, c):
        pl.semaphore_signal(
            barrier, inc=1, device_id=at(my_e, over_tensor(k)), device_id_type=MESH
        )
        return c

    def greet_expert(k, c):
        pl.semaphore_signal(
            barrier, inc=1, device_id=at(over_expert(k), my_t), device_id_type=MESH
        )
        return c

    lax.fori_loop(1, n_tensor, greet_tensor, 0)
    lax.fori_loop(1, n_expert, greet_expert, 0)

    starts, ends = [], []
    run = jnp.int32(0)
    for r in range(requests):
        starts.append(run)
        run = run + lengths_ref[r]
        ends.append(run)
    place = lax.broadcasted_iota(jnp.int32, (total, chans), 0)
    first = jnp.zeros((total, chans), jnp.int32)
    old = [conv_state[j].astype(F32) for j in range(taps - 1)]
    from_state = [jnp.zeros((total, chans), F32) for _ in range(taps - 1)]
    for r in range(requests):
        inside = place >= starts[r]
        first = jnp.where(inside, starts[r], first)
        for j in range(taps - 1):
            from_state[j] = jnp.where(inside, old[j][r : r + 1, :], from_state[j])
    since = place - first
    shifted[0:8, :] = jnp.zeros((8, chans), F32)
    shifted[8:, :] = mixer_input[...].astype(F32)
    summed = jnp.zeros((total, chans), F32) + conv_bias[...]
    for k in range(taps):
        back = taps - 1 - k
        value = shifted[8 - back : 8 - back + total, :]
        if back:
            carried_in = from_state[0]
            for j in range(1, taps - 1):
                carried_in = jnp.where(since - back + taps - 1 == j, from_state[j], carried_in)
            value = jnp.where(since >= back, value, carried_in)
        summed = summed + conv_weight[k : k + 1, :] * value
    conv_out = silu(summed).astype(BF16)
    conv_float = conv_out.astype(F32)

    partial = jnp.dot(conv_out, state_proj[...], preferred_element_type=F32)
    for t in range(n_tensor):
        part_send[t] = partial[t * rows_each : (t + 1) * rows_each, :]
    part_recv[my_t] = part_send[my_t]

    pl.semaphore_wait(barrier, n_tensor + n_expert - 2)

    def to_tensor(source, target, send, recv):
        def copy(k):
            t = over_tensor(k)
            return pltpu.make_async_remote_copy(
                src_ref=source(t),
                dst_ref=target.at[my_t],
                send_sem=send.at[k],
                recv_sem=recv.at[k],
                device_id=at(my_e, t),
                device_id_type=MESH,
            )

        return copy

    def to_expert(source, target, send, recv):
        def copy(k):
            e = over_expert(k)
            return pltpu.make_async_remote_copy(
                src_ref=source(e),
                dst_ref=target.at[my_e],
                send_sem=send.at[k],
                recv_sem=recv.at[k],
                device_id=at(e, my_t),
                device_id_type=MESH,
            )

        return copy

    def start_all(copy, count):
        for k in range(1, count):
            copy(k).start()

    def receive_all(copy, count):
        for k in range(1, count):
            copy(k).wait_recv()

    def sent_all(copy, count):
        for k in range(1, count):
            copy(k).wait_send()

    copy1 = to_tensor(lambda t: part_send.at[t], part_recv, s1, r1)
    copy2 = to_expert(lambda e: proj_send, proj_recv, s2, r2)
    copy7 = to_tensor(lambda t: proj_all.at[my_t], proj_all, s7, r7)
    start_all(copy1, n_tensor)
    receive_all(copy1, n_tensor)
    proj_send[...] = jnp.sum(part_recv[...], axis=0)
    start_all(copy2, n_expert)
    proj_recv[my_e] = proj_send[...]
    receive_all(copy2, n_expert)
    proj_all[my_t] = jnp.sum(proj_recv[...], axis=0)
    start_all(copy7, n_tensor)

    slots = []
    for w in range(EXP_WIN):
        count = jnp.int32(0)
        index = [jnp.int32(0) for _ in range(CAP)]
        weight = [jnp.float32(0) for _ in range(CAP)]
        for row in range(toks):
            zero = ids_ref[0, row] == w
            one = ids_ref[1, row] == w
            named = jnp.logical_or(zero, one)
            gate = jnp.where(zero, gates_ref[0, row], 0.0) + jnp.where(one, gates_ref[1, row], 0.0)
            for s in range(CAP):
                here = jnp.logical_and(named, count == s)
                index[s] = jnp.where(here, row, index[s])
                weight[s] = jnp.where(here, gate, weight[s])
            count = count + named.astype(jnp.int32)
        slots.append((index, weight))

    receive_all(copy7, n_tensor)
    projected = proj_all[...].reshape(total, rank + 2 * states)
    step_low = projected[:, :rank].astype(BF16)
    input_map = projected[:, rank : rank + states]
    output_map = projected[:, rank + states :]
    raw = (
        lax.dot_general(
            step_low, step_proj[...], (((1,), (1,)), ((), ())), preferred_element_type=F32
        )
        + step_bias[...]
    )
    step = jnp.maximum(raw, 0.0) + jnp.log1p(jnp.exp(-jnp.abs(raw)))

    decay_all[...] = jnp.exp(-step[:, None, :] * decay_rate[...][None, :, :])
    drive_all[...] = (step * conv_float)[:, None, :] * input_map[:, :, None]

    def advance(t, carry):
        h, r, begin, end = carry
        before = jnp.where(t == begin, ssm_state[r], h)
        h = decay_all[t] * before + drive_all[t]
        carried[t] = h
        over = t + 1 == end
        following = jnp.minimum(r + 1, requests - 1)
        return (
            h,
            jnp.where(over, following, r),
            jnp.where(over, end, begin),
            jnp.where(over, end + lengths_ref[following], end),
        )

    lax.fori_loop(
        0,
        total,
        advance,
        (jnp.zeros((states, chans), F32), jnp.int32(0), jnp.int32(0), ends[0]),
    )
    for r in range(requests):
        final_state[r] = carried[jnp.clip(ends[r] - 1, 0, total - 1)]
    scanned = jnp.sum(carried[...] * output_map[:, :, None], axis=1)
    mixed = (scanned + skip_gain[...] * conv_float) * silu(mixer_gate[...].astype(F32))
    mixed_all[my_t] = mixed.astype(BF16)

    copy3 = to_tensor(lambda t: mixed_all.at[my_t], mixed_all, s3, r3)
    start_all(copy3, n_tensor)
    receive_all(copy3, n_tensor)
    part = jnp.zeros((total, feats), F32)
    for t in range(n_tensor):
        part = part + jnp.dot(
            mixed_all[t], out_proj[t * chans : (t + 1) * chans, :], preferred_element_type=F32
        )
    half = feats // 2
    for e in range(n_expert):
        rows = part[e * toks : (e + 1) * toks, :]
        mix_send[e] = jnp.concatenate([rows[:, :half], rows[:, half:]], axis=0).astype(BF16)
    mix_recv[my_e] = mix_send[my_e]

    copy4 = to_expert(lambda e: mix_send.at[e], mix_recv, s4, r4)
    start_all(copy4, n_expert)
    receive_all(copy4, n_expert)
    mix = jnp.sum(mix_recv[...].astype(F32), axis=0)
    stream = residual[...].astype(F32) + jnp.concatenate([mix[:toks], mix[toks:]], axis=1)
    squares = jnp.sum(stream * stream, axis=1, keepdims=True)
    stream_s[:, :feats] = stream * norm_gain[...]
    stream_s[:, feats:] = jnp.broadcast_to(squares, (toks, LANES))

    for w in range(EXP_WIN):
        for s in range(CAP):
            tok_send[w, s : s + 1, :] = stream_s[pl.ds(slots[w][0][s], 1), :]
    tok_held[my_e] = tok_send[my_e // group]
    copy5 = to_expert(lambda e: tok_send.at[e // group], tok_held, s5, r5)
    start_all(copy5, n_expert)
    receive_all(copy5, n_expert)
    for e in range(n_expert):
        tok_recv[my_t, e * CAP : (e + 1) * CAP, :] = tok_held[e]
    copy8 = to_tensor(lambda t: tok_recv.at[my_t], tok_recv, s8, r8)
    start_all(copy8, n_tensor)
    receive_all(copy8, n_tensor)
    padded = tokens_s.shape[0]
    if padded > held:
        tokens_s[held:, :] = jnp.zeros((padded - held, width + LANES), F32)
    square = jnp.zeros((held, LANES), F32)
    for t in range(n_tensor):
        tokens_s[:held, t * feats : (t + 1) * feats] = tok_recv[t, :, :feats]
        square = square + tok_recv[t, :, feats:]
    tokens_s[:held, width:] = square
    scale = lax.rsqrt(tokens_s[:, width : width + 1] / width + EPSILON)
    normed = (tokens_s[:, :width] * scale).astype(BF16)

    loads[0].wait()
    loads[1].wait()
    units = gate_v.shape[1]
    tile = 256 if units % 256 == 0 else units

    def unit_tile(i, c):
        cols = pl.ds(pl.multiple_of(i * tile, tile), tile) if units > tile else slice(None)
        g = jnp.dot(normed, gate_v[:, cols], preferred_element_type=F32)
        u = jnp.dot(normed, up_v[:, cols], preferred_element_type=F32)
        hidden[:, cols] = (silu(g) * u).astype(BF16)
        return c

    lax.fori_loop(0, units // tile, unit_tile, 0)
    loads[2].wait()
    act = hidden[...]
    otile = 512 if feats % 512 == 0 else feats
    copy6 = to_tensor(lambda t: out_send.at[t], out_held, s6, r6)

    def out_block(t):
        def out_tile(i, c):
            cols = pl.ds(pl.multiple_of(i * otile, otile), otile)
            base = pl.ds(pl.multiple_of(t * feats + i * otile, otile), otile)
            got = jnp.dot(act, down_v[:, base], preferred_element_type=F32)
            out_send[t, :, cols] = got[:held]
            return c

        lax.fori_loop(0, feats // otile, out_tile, 0)

    def send_block(k, c):
        out_block(over_tensor(k))
        copy6(k).start()
        return c

    lax.fori_loop(1, n_tensor, send_block, 0)
    out_block(my_t)
    out_held[my_t] = out_send[my_t]
    receive_all(copy6, n_tensor)
    gathered = jnp.sum(out_held[...], axis=0)
    for e in range(n_expert):
        out_part[e] = gathered[e * CAP : (e + 1) * CAP, :]
    copy9 = to_expert(lambda e: out_part.at[e], out_recv, s9, r9)
    start_all(copy9, n_expert)
    out_recv[my_e] = out_part[my_e]
    receive_all(copy9, n_expert)
    row_id = lax.broadcasted_iota(jnp.int32, (toks, feats), 0)
    result = residual[...].astype(F32) + jnp.concatenate([mix[:toks], mix[toks:]], axis=1)
    for w in range(EXP_WIN):
        value = jnp.sum(out_recv[w * group : (w + 1) * group], axis=0)
        for s in range(CAP):
            index, weight = slots[w]
            result = result + jnp.where(row_id == index[s], weight[s], 0.0) * value[s : s + 1, :]
    layer_out[...] = result.astype(BF16)
    for copy, count in (
        (copy1, n_tensor),
        (copy2, n_expert),
        (copy7, n_tensor),
        (copy3, n_tensor),
        (copy4, n_expert),
        (copy5, n_expert),
        (copy8, n_tensor),
        (copy6, n_tensor),
        (copy9, n_expert),
    ):
        sent_all(copy, count)


def finish(layer_in, state_in, layer_out, final_state):
    layer_out[...] = layer_in[...]
    final_state[...] = state_in[...]


def body(
    n_expert,
    n_tensor,
    mixer_input,
    mixer_gate,
    conv_state,
    conv_weight,
    conv_bias,
    ssm_state,
    decay_rate,
    step_bias,
    skip_gain,
    state_proj,
    step_proj,
    out_proj,
    residual,
    norm_gain,
    expert_gate,
    expert_up,
    expert_down,
    expert_ids,
    route_gates,
    request_lengths,
):
    total, chans = mixer_input.shape
    states = decay_rate.shape[0]
    xw = state_proj.shape[1]
    toks, feats = residual.shape
    width = feats * n_tensor
    rows_each = total // n_tensor
    slots = n_expert * CAP
    held = -(-n_expert * CAP // 16) * 16
    smem = pl.BlockSpec(memory_space=pltpu.SMEM)
    vmem = pl.BlockSpec(memory_space=pltpu.VMEM)
    hbm = pl.BlockSpec(memory_space=pl.ANY)
    sem = pltpu.SemaphoreType.DMA
    made = pl.pallas_call(
        functools.partial(kernel, n_expert, n_tensor),
        out_shape=(
            jax.ShapeDtypeStruct((toks, feats), BF16),
            jax.ShapeDtypeStruct(ssm_state.shape, F32),
        ),
        in_specs=[smem] * 3 + [vmem] * 14 + [hbm] * 3,
        out_specs=(vmem, vmem),
        scratch_shapes=[
            pltpu.VMEM(expert_gate.shape, BF16),
            pltpu.VMEM(expert_up.shape, BF16),
            pltpu.VMEM(expert_down.shape, BF16),
            pltpu.VMEM((total + 8, chans), F32),
            pltpu.VMEM((n_tensor, rows_each, xw), F32),
            pltpu.VMEM((n_tensor, rows_each, xw), F32),
            pltpu.VMEM((rows_each, xw), F32),
            pltpu.VMEM((n_expert, rows_each, xw), F32),
            pltpu.VMEM((n_tensor, rows_each, xw), F32),
            pltpu.VMEM((total, states, chans), F32),
            pltpu.VMEM((total, states, chans), F32),
            pltpu.VMEM((total, states, chans), F32),
            pltpu.VMEM((n_tensor, total, chans), BF16),
            pltpu.VMEM((n_expert, 2 * toks, feats // 2), BF16),
            pltpu.VMEM((n_expert, 2 * toks, feats // 2), BF16),
            pltpu.VMEM((toks, feats + LANES), F32),
            pltpu.VMEM((EXP_WIN, CAP, feats + LANES), F32),
            pltpu.VMEM((n_expert, CAP, feats + LANES), F32),
            pltpu.VMEM((n_tensor, slots, feats + LANES), F32),
            pltpu.VMEM((held, width + LANES), F32),
            pltpu.VMEM((held, expert_gate.shape[1]), BF16),
            pltpu.VMEM((n_tensor, slots, feats), F32),
            pltpu.VMEM((n_tensor, slots, feats), F32),
            pltpu.VMEM((n_expert, CAP, feats), F32),
            pltpu.VMEM((n_expert, CAP, feats), F32),
            sem((3,)),
            sem((n_tensor,)),
            sem((n_tensor,)),
            sem((n_expert,)),
            sem((n_expert,)),
            sem((n_tensor,)),
            sem((n_tensor,)),
            sem((n_expert,)),
            sem((n_expert,)),
            sem((n_expert,)),
            sem((n_expert,)),
            sem((n_tensor,)),
            sem((n_tensor,)),
            sem((n_tensor,)),
            sem((n_tensor,)),
            sem((n_tensor,)),
            sem((n_tensor,)),
            sem((n_expert,)),
            sem((n_expert,)),
        ],
        compiler_params=pltpu.CompilerParams(
            collective_id=0, has_side_effects=True, vmem_limit_bytes=60 * 1024 * 1024
        ),
    )(
        request_lengths,
        expert_ids.T,
        route_gates.T,
        mixer_input,
        mixer_gate,
        conv_state.transpose(1, 0, 2),
        conv_weight,
        conv_bias[None],
        ssm_state,
        decay_rate,
        step_bias[None],
        skip_gain[None],
        state_proj,
        step_proj.T,
        out_proj,
        residual,
        norm_gain[None],
        expert_gate,
        expert_up,
        expert_down,
    )
    return pl.pallas_call(
        finish,
        out_shape=tuple(jax.ShapeDtypeStruct(m.shape, m.dtype) for m in made),
        in_specs=[vmem] * 2,
        out_specs=(vmem, vmem),
    )(*made)


def solution(mesh):
    in_specs = (
        P("groups", ("expert", "tensor")),
        P("groups", ("expert", "tensor")),
        P("groups", None, ("expert", "tensor")),
        P(None, ("expert", "tensor")),
        P(("expert", "tensor")),
        P("groups", None, ("expert", "tensor")),
        P(None, ("expert", "tensor")),
        P(("expert", "tensor")),
        P(("expert", "tensor")),
        P(("expert", "tensor"), None),
        P(None, ("expert", "tensor")),
        P("expert", "tensor"),
        P(("groups", "expert"), "tensor"),
        P("tensor"),
        P(None, ("expert", "tensor")),
        P(None, ("expert", "tensor")),
        P(("expert", "tensor"), None),
        P(("groups", "expert"), None),
        P(("groups", "expert"), None),
        P("groups"),
    )
    out_specs = (P(("groups", "expert"), "tensor"), P("groups", None, ("expert", "tensor")))
    run = functools.partial(body, mesh.shape["expert"], mesh.shape["tensor"])
    return jax.shard_map(run, mesh=mesh, in_specs=in_specs, out_specs=out_specs, check_vma=False)
```
